32 devices in a mesh: groups: 2 (over y), seq: 4 (over z), req: 2 (over x), head: 2 (over core).
Axes of the slice: x: 2, y: 2, z: 4, core: 2. Of those that a mesh axis runs over, the one named last changes fastest.
Arguments:
- cache: bfloat16 [8, 6144, 576], P(('groups', 'req'), 'seq'), parts along dimension 0, may hold values from -4 to 4
- index_key: bfloat16 [8, 6144, 128], P(('groups', 'req'), 'seq'), parts along dimension 0, may hold values from -4 to 4
- index_scale: float32 [8, 6144], P(('groups', 'req'), 'seq'), parts along dimension 0, may hold values from 1.5 to 12
- lengths: int32 [8], P(('groups', 'req')), parts along dimension 0, may hold values from 4608 to 6143, as said below
- owners: int32 [8], P(('groups', 'req')), parts along dimension 0, may hold values from 0 to 3, as said below
- selected: int32 [2, 8, 2048], P(None, ('groups', 'req')), parts along dimension 1, may hold values from 0 to 6143, as said below
- query: bfloat16 [2, 16, 128, 576], P(None, ('groups', 'seq', 'req'), 'head'), parts along dimension 1, may hold values from -41 to 41
- index_query: bfloat16 [2, 16, 64, 128], P(None, ('groups', 'seq', 'req')), parts along dimension 1, may hold values from -0.5 to 0.5
- index_weight: bfloat16 [2, 16, 64], P(None, ('groups', 'seq', 'req')), parts along dimension 1, may hold values from -0.75 to 0.75
Outputs:
- index_scores: float32 [2, 8, 6144], P(None, ('groups', 'req'), 'seq'), parts along dimension 1
- threshold: float32 [2, 8], P(None, ('groups', 'req')), parts along dimension 1
- attended: bfloat16 [2, 16, 128, 512], P(None, ('groups', 'seq', 'req'), 'head'), parts along dimension 1
The draws below stay inside these ranges and needn't reach their ends.
There are 2 independent parts, one for each index of `groups`. The reference program is written for one: setup_inputs(seed, part) draws one part's arguments, and reference() takes and returns one part's arrays. A program takes and returns all parts, laid end to end along the dimension named above; each array names one. Nothing has to cross between parts.
Inputs may be any that keep to these rules, and one draw needn't show every extreme that they name: `lengths`: some request of each group has length 6143. The 2 requests i * 2 to (i + 1) * 2 - 1 have distinct owners. selected[t, r] holds 2048 distinct positions below lengths[r] + t; at most 768 of them lie in one block of positions k * 1536 to (k + 1) * 1536 - 1, and in every list some block holds exactly 768.
All inputs are finite; a program needn't handle non-finite values.
Results may differ from the reference program's by a relative error of at most 0.007.
Values may be sent and summed in bfloat16 or wider, within the bound.
A program may use at most 64 MiB of HBM per device.

```python
import math
import jax
import jax.numpy as jnp
from jax import lax

H = 128
LAT = 512
ROPE = 64
IH = 64
IDK = 128
TOPK = 2048
CTX = 6144
STEPS = 2
REQ_COL = 2
REQS = 4
SH = 1536
CAP = 768
LEN_MIN = 4608
SLOTS = 8
N_SEQ = 4
N_REQ = 2


def length_draw(key):
    spread = jax.random.randint(jax.random.fold_in(key, 101), (REQS,), LEN_MIN, CTX)
    order = jax.random.permutation(jax.random.fold_in(key, 102), REQS)
    spread = spread.at[order[0]].set(CTX - 1)
    spread = spread.at[order[1]].set(LEN_MIN)
    return spread.astype(jnp.int32)


def owner_draw(key):
    column_keys = jax.random.split(jax.random.fold_in(key, 201), N_REQ)

    def column(subkey):
        return jax.random.permutation(subkey, N_SEQ)[:REQ_COL]
    return jax.vmap(column)(column_keys).reshape(REQS).astype(jnp.int32)


def one_list(list_key, length):
    full = length // SH
    heavy_key, perm_key, order_key = jax.random.split(list_key, 3)
    heavy = jax.random.randint(heavy_key, (), 0, full)
    shard = jnp.arange(N_SEQ, dtype=jnp.int32)
    rest = TOPK - CAP
    base_count = rest // (full - 1)
    extra = rest % (full - 1)
    among = shard - (shard > heavy).astype(jnp.int32)
    counts = jnp.where(shard == heavy, CAP, jnp.where(shard < full, base_count + (among < extra).astype(jnp.int32), 0))
    perm_keys = jax.random.split(perm_key, N_SEQ)
    perms = jax.vmap(lambda subkey: jax.random.permutation(subkey, SH))(perm_keys)
    ranks = jnp.argsort(perms, axis=1)
    chosen = (ranks < counts[:, None]).reshape(CTX)
    picked = jnp.nonzero(chosen, size=TOPK, fill_value=0)[0]
    return picked[jax.random.permutation(order_key, TOPK)].astype(jnp.int32)


def selection_draw(key):
    lengths = length_draw(key)
    list_keys = jax.random.split(jax.random.fold_in(key, 301), STEPS * REQS)
    step_lengths = lengths[None, :] + jnp.arange(STEPS, dtype=jnp.int32)[:, None]
    lists = jax.vmap(one_list)(list_keys, step_lengths.reshape(STEPS * REQS))
    return lists.reshape(STEPS, REQS, TOPK)


def cache_rows(key, flat_index):
    base_key = jax.random.fold_in(key, 401)

    def row_draw(index):
        row_key = jax.random.fold_in(base_key, index)
        values = jnp.clip(jax.random.normal(row_key, (LAT + ROPE,)), -4.0, 4.0)
        return values.astype(jnp.bfloat16).astype(jnp.float32)
    rows = jax.vmap(row_draw)(flat_index.reshape(-1))
    return rows.reshape(flat_index.shape + (LAT + ROPE,))


def draw_cache(key, part):
    rows = cache_rows(key, jnp.arange(REQS * CTX, dtype=jnp.int32))
    return rows.reshape(REQS, CTX, LAT + ROPE).astype(jnp.bfloat16)


def draw_lengths(key, part):
    return length_draw(key)


def draw_owners(key, part):
    return owner_draw(key)


def draw_selected(key, part):
    return selection_draw(key)


def draw_query(key, part):
    shape = (STEPS, SLOTS, H, LAT + ROPE)
    values = jnp.clip(1.2 * jax.random.normal(jax.random.fold_in(key, 501), shape), -4.8, 4.8)
    return values.astype(jnp.bfloat16)


def levels(rng, extent, cuts, smallest, high):
    loudness, own = 1.0, jax.random.fold_in(rng, 6)
    for dim, parts in cuts:
        heights = jnp.exp(jax.random.uniform(jax.random.fold_in(own, dim), (parts,), jnp.float32, smallest / len(cuts), high / len(cuts)))
        loudness = loudness * jnp.repeat(heights, extent[dim] // parts).reshape([-1 if axis == dim else 1 for axis in range(len(extent))])
    return loudness


def centred(rng, dims, deviation, bound, pieces=(), kind=jnp.bfloat16):
    values = deviation * jax.random.normal(rng, dims, jnp.float32)
    if pieces:
        values = values * levels(rng, dims, pieces, -0.22, 0.18)
    return jnp.clip(values, -bound, bound).astype(kind)


def setup_inputs(seed: int = 0, part: int = 0) -> dict:
    keys = jax.random.split(jax.random.key(seed), 10)
    part_keys = jax.random.split(jax.random.fold_in(keys[9], part), 10)
    return {
        "cache": draw_cache(jax.random.fold_in(jax.random.fold_in(keys[9], part), 71), part),
        "index_key": centred(part_keys[1], (REQS, CTX, IDK), 1.0, 4.0, ((0, 2), (1, 4))),
        "index_scale": jnp.clip(jnp.exp(math.log(12.0) - 2.0794415 * jax.random.uniform(part_keys[2], (REQS, CTX), jnp.float32) ** levels(part_keys[2], (REQS, CTX), ((0, 2), (1, 4)), -0.2, 0.2)), 1.5, 12.0),
        "lengths": draw_lengths(jax.random.fold_in(jax.random.fold_in(keys[9], part), 71), part),
        "owners": draw_owners(jax.random.fold_in(jax.random.fold_in(keys[9], part), 71), part),
        "selected": draw_selected(jax.random.fold_in(jax.random.fold_in(keys[9], part), 71), part),
        "query": draw_query(jax.random.fold_in(jax.random.fold_in(keys[9], part), 71), part),
        "index_query": centred(part_keys[7], (STEPS, SLOTS, IH, IDK), IDK ** -0.5, 0.5, ((1, 8),)),
        "index_weight": centred(part_keys[8], (STEPS, SLOTS, IH), IH ** -0.5, 0.75, ((1, 8),)),
    }


score_scale = 192.0 ** -0.5
masked_value = -1.0e30


def reference(cache, index_key, index_scale, lengths, owners, selected, query, index_query, index_weight):
    requests = jnp.arange(REQS, dtype=jnp.int32)
    slot_of = (owners * N_REQ + requests // REQ_COL).astype(jnp.int32)
    positions = jnp.arange(CTX, dtype=jnp.int32)

    def per_request(request):
        slot_index = slot_of[request]
        index_rows = index_key[request]
        request_rows = cache[request]
        length = lengths[request]
        score_list = []
        top_list = []
        output_list = []
        for step_index in range(STEPS):
            heads_query = index_query[step_index, slot_index]
            raw_dots = jnp.dot(heads_query, index_rows.T, preferred_element_type=jnp.float32)
            head_weight = index_weight[step_index, slot_index].astype(jnp.float32)
            weighted = jnp.sum(jax.nn.relu(raw_dots) * head_weight[:, None], axis=0)
            scores = weighted * index_scale[request]
            in_length = positions < length + step_index
            score_list.append(jnp.where(in_length, scores, 0.0))
            ranked = lax.top_k(jnp.where(in_length, scores, masked_value), TOPK)[0]
            top_list.append(ranked[TOPK - 1])
            picked_rows = jnp.take(request_rows, selected[step_index, request], axis=0)
            logits = jnp.dot(query[step_index, slot_index], picked_rows.T, preferred_element_type=jnp.float32) * score_scale
            row_peak = jnp.max(logits, axis=1, keepdims=True)
            weights = jnp.exp(logits - row_peak)
            row_total = jnp.sum(weights, axis=1, keepdims=True)
            mixture = jnp.dot(weights.astype(jnp.bfloat16), picked_rows[:, :LAT], preferred_element_type=jnp.float32)
            output_list.append((mixture / row_total).astype(jnp.bfloat16))
        return jnp.stack(score_list), jnp.stack(top_list), jnp.stack(output_list)

    all_scores, all_tops, outputs = lax.map(per_request, requests)
    attended = jnp.zeros((STEPS, SLOTS, H, LAT), jnp.bfloat16)
    attended = attended.at[:, slot_of].set(jnp.transpose(outputs, (1, 0, 2, 3)))
    return jnp.transpose(all_scores, (1, 0, 2)), jnp.transpose(all_tops, (1, 0)), attended
```

```python
import functools

import jax
import jax.numpy as jnp
from jax import lax
from jax.experimental import pallas as pl
from jax.experimental.pallas import tpu as pltpu
from jax.sharding import PartitionSpec as P

ROPE = 64
LANES = 128
PIVOTS = 7
ROUNDS = 11

score_scale = 192.0 ** (-0.5)
masked_value = -1e30
NT = (((1,), (1,)), ((), ()))
NN = (((1,), (0,)), ((), ()))


def dot(a, b, dims):
    return lax.dot_general(a, b, dims, preferred_element_type=jnp.float32)


def iota(shape, dim):
    return lax.broadcasted_iota(jnp.int32, shape, dim)


def to_column(row):
    n = row.shape[1]
    eye = iota((n, n), 0) == iota((n, n), 1)
    return jnp.sum(jnp.where(eye, row, 0.0), axis=1, keepdims=True)


def to_row(column):
    n = column.shape[0]
    eye = iota((n, n), 0) == iota((n, n), 1)
    return jnp.sum(jnp.where(eye, column, 0.0), axis=0, keepdims=True)


def kernel(
    n,
    lengths,
    owners,
    cache_hbm,
    key_hbm,
    scale_ref,
    selected_ref,
    query_ref,
    iq_ref,
    iw_ref,
    scores_out,
    threshold_out,
    attended_out,
    cache_v,
    key_v,
    iq_all,
    q_all,
    cand,
    bias,
    mix_out,
    stat_out,
    mix_in,
    stat_in,
    local_sem,
    iq_send,
    iq_recv,
    q_send,
    q_recv,
    c_send,
    c_recv,
    m_send,
    m_recv,
    s_send,
    s_recv,
):
    me = lax.axis_index("seq")
    steps, reqs, picks = selected_ref.shape
    rows = cache_v.shape[1]
    heads = query_ref.shape[2]
    latent = mix_in.shape[2]
    iheads = iq_ref.shape[2]
    crow = cand.shape[1]
    fold = crow // (steps * reqs)

    key_copy = pltpu.make_async_copy(key_hbm, key_v, local_sem.at[0])
    cache_copy = pltpu.make_async_copy(cache_hbm, cache_v, local_sem.at[1])
    key_copy.start()
    cache_copy.start()

    def peer(d):
        return lax.rem(me + d, n)

    def remote(src, dst, send, recv, d):
        return pltpu.make_async_remote_copy(
            src_ref=src,
            dst_ref=dst,
            send_sem=send.at[peer(d)],
            recv_sem=recv,
            device_id={"seq": peer(d)},
            device_id_type=pl.DeviceIdType.MESH,
        )

    barrier = pltpu.get_barrier_semaphore()
    for d in range(1, n):
        pl.semaphore_signal(
            barrier, inc=1, device_id={"seq": peer(d)}, device_id_type=pl.DeviceIdType.MESH
        )
    for t in range(steps):
        iq_all[me, t * iheads : (t + 1) * iheads, :] = iq_ref[t, 0]
    wide = jnp.concatenate([iw_ref[t] for t in range(steps)], axis=0).astype(jnp.float32)
    iq_all[me, steps * iheads :, :] = jnp.pad(
        wide, ((0, 16 - steps), (0, LANES - iheads))
    ).astype(jnp.bfloat16)
    q_all[me] = query_ref[:, 0]
    pl.semaphore_wait(barrier, n - 1)

    for d in range(1, n):
        remote(iq_all.at[me], iq_all.at[me], iq_send, iq_recv.at[me], d).start()
    for d in range(1, n):
        remote(q_all.at[me], q_all.at[me], q_send, q_recv.at[me], d).start()

    base = me * rows
    blocks = rows // LANES
    hi_rows = -(-blocks // 16) * 16
    for j in range(reqs):
        for t in range(steps):
            local = selected_ref[t, j : j + 1, :] - base
            hi = jnp.right_shift(local, 7)
            lo = jnp.bitwise_and(local, LANES - 1)
            hot_hi = jnp.where(iota((hi_rows, picks), 0) == hi, 1.0, 0.0).astype(jnp.bfloat16)
            hot_lo = jnp.where(iota((LANES, picks), 0) == lo, 1.0, 0.0).astype(jnp.bfloat16)
            hits = dot(hot_hi, hot_lo, NT)
            row = jnp.concatenate([hits[b : b + 1] for b in range(blocks)], axis=1)
            bias[j, t : t + 1, :] = jnp.where(row > 0.5, 0.0, masked_value)

    key_copy.wait()
    for d in range(1, n):
        remote(iq_all.at[peer(d)], iq_all.at[peer(d)], iq_send, iq_recv.at[peer(d)], d).wait_recv()
    position = base + iota((1, rows), 1)
    part = rows // fold
    for j in range(reqs):
        packed = iq_all[owners[j]]
        dots = jnp.maximum(dot(packed[: steps * iheads], key_v[j], NT), 0.0)
        scale = scale_ref[j : j + 1, :]
        for t in range(steps):
            w = packed[steps * iheads :].astype(jnp.float32)[t : t + 1, :iheads]
            total = jnp.sum(
                dots[t * iheads : (t + 1) * iheads] * to_column(w), axis=0, keepdims=True
            )
            total = total * scale
            inside = position < lengths[j] + t
            scores_out[t, j : j + 1, :] = jnp.where(inside, total, 0.0)
            candidates = jnp.where(inside, total, masked_value)
            for f in range(fold):
                at = f * steps * reqs + t * reqs + j
                cand[me, at : at + 1, :] = candidates[:, f * part : (f + 1) * part]
    for d in range(1, n):
        remote(cand.at[me], cand.at[me], c_send, c_recv.at[me], d).start()

    cache_copy.wait()

    def unit(s):
        j = jnp.int32(0)
        for r in range(reqs):
            j = j + jnp.where(owners[r] == s, r, 0)
        latents = cache_v[j]
        logits = dot(q_all[s].reshape(steps * heads, -1), latents, NT) * score_scale
        mask = bias[j]
        logits = jnp.concatenate(
            [logits[t * heads : (t + 1) * heads] + mask[t : t + 1] for t in range(steps)], axis=0
        )
        peak = jnp.max(logits, axis=1, keepdims=True)
        weights = jnp.exp(logits - peak)
        total = jnp.sum(weights, axis=1, keepdims=True)
        mixture = dot(weights.astype(jnp.bfloat16), latents[:, :latent], NN) / total
        stat = jnp.concatenate([to_row(peak), to_row(total)], axis=0)
        return mixture.astype(jnp.bfloat16), jnp.pad(stat, ((0, 6), (0, 0)))

    mix_in[me], stat_in[me] = unit(me)

    def send_unit(d, carry):
        s = peer(d)
        remote(q_all.at[s], q_all.at[s], q_send, q_recv.at[s], d).wait_recv()
        mix_out[s], stat_out[s] = unit(s)
        remote(mix_out.at[s], mix_in.at[me], m_send, m_recv.at[me], d).start()
        remote(stat_out.at[s], stat_in.at[me], s_send, s_recv.at[me], d).start()
        return carry

    lax.fori_loop(1, n, send_unit, 0)

    for d in range(1, n):
        remote(cand.at[peer(d)], cand.at[peer(d)], c_send, c_recv.at[peer(d)], d).wait_recv()
    values = [cand[s] for s in range(n)]

    def across(x, join):
        for f in range(1, fold):
            x = join(x, pltpu.roll(x, f * steps * reqs, 0))
        return x

    def folded(parts, join, reduce):
        x = functools.reduce(join, parts)
        pieces = [x[:, i * LANES : (i + 1) * LANES] for i in range(part // LANES)]
        x = reduce(functools.reduce(join, pieces), axis=1, keepdims=True)
        return across(jnp.broadcast_to(x, (crow, LANES)), join)

    def tile(x):
        return jnp.tile(x, (1, part // LANES))

    highest = folded(values, jnp.maximum, jnp.max)
    lowest = folded(
        [jnp.where(v > 0.5 * masked_value, v, -masked_value) for v in values], jnp.minimum, jnp.min
    )

    def search(_, state):
        low, high = state
        step = (high - low) * (1.0 / (PIVOTS + 1))
        pivots = [low + step * i for i in range(1, PIVOTS + 1)]
        new_low, new_high = low, high
        enough = []
        for pivot in pivots:
            wide_pivot = tile(pivot)
            count = folded(
                [jnp.where(v >= wide_pivot, 1.0, 0.0) for v in values], jnp.add, jnp.sum
            )
            enough.append(count >= picks)
        for pivot, yes in zip(pivots, enough):
            new_low = jnp.where(yes, pivot, new_low)
        for pivot, yes in reversed(list(zip(pivots, enough))):
            new_high = jnp.where(yes, new_high, pivot)
        return new_low, new_high

    low, _ = lax.fori_loop(0, ROUNDS, search, (lowest, highest))
    wide_low = tile(low)
    found = folded(
        [jnp.where(v >= wide_low, v, -masked_value) for v in values], jnp.minimum, jnp.min
    )
    column = found[:, :1]
    for t in range(steps):
        hit = iota((crow, reqs), 0) == t * reqs + iota((crow, reqs), 1)
        threshold_out[t : t + 1, :] = jnp.sum(jnp.where(hit, column, 0.0), axis=0, keepdims=True)

    for d in range(1, n):
        s = peer(d)
        remote(stat_in.at[s], stat_in.at[s], s_send, s_recv.at[s], d).wait_recv()
        remote(mix_in.at[s], mix_in.at[s], m_send, m_recv.at[s], d).wait_recv()
    peaks = [stat_in[s, 0:1, :] for s in range(n)]
    top = functools.reduce(jnp.maximum, peaks)
    shares = [stat_in[s, 1:2, :] * jnp.exp(peaks[s] - top) for s in range(n)]
    whole = functools.reduce(jnp.add, shares)
    held = jnp.int32(0)
    for r in range(reqs):
        held = held + jnp.where(owners[r] == me, 1, 0)
    keep = jnp.where(held > 0, 1.0, 0.0)
    merged = jnp.zeros((steps * heads, latent), jnp.float32)
    for s in range(n):
        merged = merged + mix_in[s].astype(jnp.float32) * to_column(shares[s] * keep / whole)
    result = merged.astype(jnp.bfloat16)
    for t in range(steps):
        attended_out[t, 0] = result[t * heads : (t + 1) * heads]

    for d in range(1, n):
        s = peer(d)
        remote(iq_all.at[me], iq_all.at[me], iq_send, iq_recv.at[me], d).wait_send()
        remote(q_all.at[me], q_all.at[me], q_send, q_recv.at[me], d).wait_send()
        remote(cand.at[me], cand.at[me], c_send, c_recv.at[me], d).wait_send()
        remote(mix_out.at[s], mix_in.at[me], m_send, m_recv.at[me], d).wait_send()
        remote(stat_out.at[s], stat_in.at[me], s_send, s_recv.at[me], d).wait_send()


def shards(
    cache, index_key, index_scale, lengths, owners, selected, query, index_query, index_weight
):
    n = lax.axis_size("seq")
    reqs, rows, width = cache.shape
    steps = selected.shape[0]
    heads = query.shape[2]
    iheads, idk = index_query.shape[2:]
    latent = width - ROPE
    fold = max(1, 8 // (steps * reqs))
    f32, bf16 = jnp.float32, jnp.bfloat16
    sems = [pltpu.SemaphoreType.DMA((2,))] + [pltpu.SemaphoreType.DMA((n,))] * 10
    vmem = pl.BlockSpec(memory_space=pltpu.VMEM)
    smem = pl.BlockSpec(memory_space=pltpu.SMEM)
    hbm = pl.BlockSpec(memory_space=pl.ANY)
    out = pl.pallas_call(
        functools.partial(kernel, n),
        out_shape=(
            jax.ShapeDtypeStruct((steps, reqs, rows), f32),
            jax.ShapeDtypeStruct((steps, reqs), f32),
            jax.ShapeDtypeStruct((steps, 1, heads, latent), bf16),
        ),
        in_specs=[smem, smem, hbm, hbm, vmem, vmem, vmem, vmem, vmem],
        out_specs=(vmem, vmem, vmem),
        scratch_shapes=[
            pltpu.VMEM((reqs, rows, width), bf16),
            pltpu.VMEM((reqs, rows, idk), bf16),
            pltpu.VMEM((n, steps * iheads + 16, idk), bf16),
            pltpu.VMEM((n, steps, heads, width), bf16),
            pltpu.VMEM((n, fold * steps * reqs, rows // fold), f32),
            pltpu.VMEM((reqs, steps, rows), f32),
            pltpu.VMEM((n, steps * heads, latent), bf16),
            pltpu.VMEM((n, 8, steps * heads), f32),
            pltpu.VMEM((n, steps * heads, latent), bf16),
            pltpu.VMEM((n, 8, steps * heads), f32),
        ]
        + sems,
        compiler_params=pltpu.CompilerParams(
            collective_id=0, has_side_effects=True, vmem_limit_bytes=40 * 2**20
        ),
    )(
        lengths, owners, cache, index_key, index_scale, selected, query, index_query, index_weight
    )
    return out


def solution(mesh):
    placed = (
        P(("groups", "req"), "seq", None),
        P(("groups", "req"), "seq", None),
        P(("groups", "req"), "seq"),
        P(("groups", "req")),
        P(("groups", "req")),
        P(None, ("groups", "req"), None),
        P(None, ("groups", "seq", "req"), "head", None),
        P(None, ("groups", "seq", "req"), None, None),
        P(None, ("groups", "seq", "req"), None),
    )
    return jax.shard_map(
        shards,
        mesh=mesh,
        in_specs=placed,
        out_specs=(
            P(None, ("groups", "req"), "seq"),
            P(None, ("groups", "req")),
            P(None, ("groups", "seq", "req"), "head", None),
        ),
        check_vma=False,
    )
```

```python
import functools

import jax
import jax.numpy as jnp
from jax import lax
from jax.experimental import pallas as pl
from jax.experimental.pallas import tpu as pltpu
from jax.sharding import PartitionSpec as P

ROPE = 64
LANES = 128
PIVOTS = 7
ROUNDS = 11

score_scale = 192.0 ** (-0.5)
masked_value = -1e30
NT = (((1,), (1,)), ((), ()))
NN = (((1,), (0,)), ((), ()))


def dot(a, b, dims):
    return lax.dot_general(a, b, dims, preferred_element_type=jnp.float32)


def iota(shape, dim):
    return lax.broadcasted_iota(jnp.int32, shape, dim)


def to_column(row):
    n = row.shape[1]
    eye = iota((n, n), 0) == iota((n, n), 1)
    return jnp.sum(jnp.where(eye, row, 0.0), axis=1, keepdims=True)


def to_row(column):
    n = column.shape[0]
    eye = iota((n, n), 0) == iota((n, n), 1)
    return jnp.sum(jnp.where(eye, column, 0.0), axis=0, keepdims=True)


def kernel(
    n,
    lengths,
    owners,
    cache_hbm,
    key_hbm,
    scale_ref,
    selected_ref,
    query_ref,
    iq_ref,
    iw_ref,
    scores_out,
    threshold_out,
    attended_out,
    cache_v,
    key_v,
    iq_all,
    q_all,
    cand,
    bias,
    mix_out,
    stat_out,
    mix_in,
    stat_in,
    local_sem,
    iq_send,
    iq_recv,
    q_send,
    q_recv,
    c_send,
    c_recv,
    m_send,
    m_recv,
    s_send,
    s_recv,
):
    me = lax.axis_index("seq")
    steps, reqs, picks = selected_ref.shape
    rows = cache_v.shape[2]
    heads = query_ref.shape[2]
    latent = mix_in.shape[2]
    iheads = iq_ref.shape[2]
    crow = cand.shape[1]
    fold = crow // (steps * reqs)

    key_copy = pltpu.make_async_copy(key_hbm, key_v, local_sem.at[0])
    cache_copy = pltpu.make_async_copy(cache_hbm, cache_v, local_sem.at[1])
    key_copy.start()
    cache_copy.start()

    def peer(d):
        return lax.rem(me + d, n)

    def remote(src, dst, send, recv, d):
        return pltpu.make_async_remote_copy(
            src_ref=src,
            dst_ref=dst,
            send_sem=send.at[peer(d)],
            recv_sem=recv,
            device_id={"seq": peer(d)},
            device_id_type=pl.DeviceIdType.MESH,
        )

    barrier = pltpu.get_barrier_semaphore()
    for d in range(1, n):
        pl.semaphore_signal(
            barrier, inc=1, device_id={"seq": peer(d)}, device_id_type=pl.DeviceIdType.MESH
        )
    for t in range(steps):
        iq_all[me, t * iheads : (t + 1) * iheads, :] = iq_ref[t, 0]
    wide = iw_ref[...].astype(jnp.float32)
    iq_all[me, steps * iheads :, :] = jnp.pad(
        wide, ((0, 16 - steps), (0, LANES - iheads))
    ).astype(jnp.bfloat16)
    q_all[me] = query_ref[:, 0]
    pl.semaphore_wait(barrier, n - 1)

    for d in range(1, n):
        remote(iq_all.at[me], iq_all.at[me], iq_send, iq_recv.at[me], d).start()
    for d in range(1, n):
        remote(q_all.at[me], q_all.at[me], q_send, q_recv.at[me], d).start()

    base = me * rows
    blocks = rows // LANES
    hi_rows = -(-blocks // 16) * 16
    for j in range(reqs):
        for t in range(steps):
            local = selected_ref[t, j : j + 1, :] - base
            hi = jnp.right_shift(local, 7)
            lo = jnp.bitwise_and(local, LANES - 1)
            hot_hi = jnp.where(iota((hi_rows, picks), 0) == hi, 1.0, 0.0).astype(jnp.bfloat16)
            hot_lo = jnp.where(iota((LANES, picks), 0) == lo, 1.0, 0.0).astype(jnp.bfloat16)
            hits = dot(hot_hi, hot_lo, NT)
            row = jnp.concatenate([hits[b : b + 1] for b in range(blocks)], axis=1)
            bias[j, t : t + 1, :] = jnp.where(row > 0.5, 0.0, masked_value)

    key_copy.wait()
    for d in range(1, n):
        remote(iq_all.at[peer(d)], iq_all.at[peer(d)], iq_send, iq_recv.at[peer(d)], d).wait_recv()
    position = base + iota((1, rows), 1)
    part = rows // fold
    pieces = {}
    for j in range(reqs):
        packed = iq_all[owners[j]]
        dots = jnp.maximum(dot(packed[: steps * iheads], key_v[j], NT), 0.0)
        scale = scale_ref[j : j + 1, :]
        for t in range(steps):
            w = packed[steps * iheads :].astype(jnp.float32)[t : t + 1, :iheads]
            total = jnp.sum(
                dots[t * iheads : (t + 1) * iheads] * to_column(w), axis=0, keepdims=True
            )
            total = total * scale
            inside = position < lengths[j] + t
            scores_out[t, j : j + 1, :] = jnp.where(inside, total, 0.0)
            candidates = jnp.where(inside, total, masked_value)
            for f in range(fold):
                pieces[f * steps * reqs + t * reqs + j] = candidates[:, f * part : (f + 1) * part]
    ordered = [pieces[i] for i in range(crow)]
    cand[me] = jnp.concatenate(ordered, axis=0).astype(jnp.bfloat16)
    for d in range(1, n):
        remote(cand.at[me], cand.at[me], c_send, c_recv.at[me], d).start()

    cache_copy.wait()

    def unit(s):
        j = jnp.int32(0)
        for r in range(reqs):
            j = j + jnp.where(owners[r] == s, r, 0)
        latents = cache_v[j]
        logits = dot(q_all[s].reshape(steps * heads, -1), latents, NN) * score_scale
        mask = bias[j]
        logits = jnp.concatenate(
            [logits[t * heads : (t + 1) * heads] + mask[t : t + 1] for t in range(steps)], axis=0
        )
        peak = jnp.max(logits, axis=1, keepdims=True)
        weights = jnp.exp(logits - peak)
        total = jnp.sum(weights, axis=1, keepdims=True)
        mixture = dot(weights.astype(jnp.bfloat16), latents[:latent], NT) / total
        stat = jnp.concatenate([to_row(peak), to_row(total)], axis=0)
        return mixture.astype(jnp.bfloat16), jnp.pad(stat, ((0, 6), (0, 0)))

    mix_in[me], stat_in[me] = unit(me)

    def send_unit(d, carry):
        s = peer(d)
        remote(q_all.at[s], q_all.at[s], q_send, q_recv.at[s], d).wait_recv()
        mix_out[s], stat_out[s] = unit(s)
        remote(mix_out.at[s], mix_in.at[me], m_send, m_recv.at[me], d).start()
        remote(stat_out.at[s], stat_in.at[me], s_send, s_recv.at[me], d).start()
        return carry

    lax.fori_loop(1, n, send_unit, 0)

    for d in range(1, n):
        remote(cand.at[peer(d)], cand.at[peer(d)], c_send, c_recv.at[peer(d)], d).wait_recv()
    values = [cand[s].astype(jnp.float32) for s in range(n)]

    def across(x, join):
        own = x
        for f in range(1, fold):
            x = join(x, pltpu.roll(own, f * steps * reqs, 0))
        return x

    def folded(parts, join, reduce):
        x = functools.reduce(join, parts)
        pieces = [x[:, i * LANES : (i + 1) * LANES] for i in range(part // LANES)]
        x = reduce(functools.reduce(join, pieces), axis=1, keepdims=True)
        return across(jnp.broadcast_to(x, (crow, LANES)), join)

    def tile(x):
        return jnp.tile(x, (1, part // LANES))

    highest = folded(values, jnp.maximum, jnp.max)
    lowest = folded(
        [jnp.where(v > 0.5 * masked_value, v, -masked_value) for v in values], jnp.minimum, jnp.min
    )

    def search(_, state):
        low, high = state
        step = (high - low) * (1.0 / (PIVOTS + 1))
        pivots = [low + step * i for i in range(1, PIVOTS + 1)]
        new_low, new_high = low, high
        enough = []
        for pivot in pivots:
            wide_pivot = tile(pivot)
            count = folded(
                [jnp.where(v >= wide_pivot, 1.0, 0.0) for v in values], jnp.add, jnp.sum
            )
            enough.append(count >= picks)
        for pivot, yes in zip(pivots, enough):
            new_low = jnp.where(yes, pivot, new_low)
        for pivot, yes in reversed(list(zip(pivots, enough))):
            new_high = jnp.where(yes, new_high, pivot)
        return new_low, new_high

    low, _ = lax.fori_loop(0, ROUNDS, search, (lowest, highest))
    wide_low = tile(low)
    found = folded(
        [jnp.where(v >= wide_low, v, -masked_value) for v in values], jnp.minimum, jnp.min
    )
    column = found[:, :1]
    for t in range(steps):
        hit = iota((crow, reqs), 0) == t * reqs + iota((crow, reqs), 1)
        threshold_out[t : t + 1, :] = jnp.sum(jnp.where(hit, column, 0.0), axis=0, keepdims=True)

    for d in range(1, n):
        s = peer(d)
        remote(stat_in.at[s], stat_in.at[s], s_send, s_recv.at[s], d).wait_recv()
        remote(mix_in.at[s], mix_in.at[s], m_send, m_recv.at[s], d).wait_recv()
    peaks = [stat_in[s, 0:1, :] for s in range(n)]
    top = functools.reduce(jnp.maximum, peaks)
    shares = [stat_in[s, 1:2, :] * jnp.exp(peaks[s] - top) for s in range(n)]
    whole = functools.reduce(jnp.add, shares)
    held = jnp.int32(0)
    for r in range(reqs):
        held = held + jnp.where(owners[r] == me, 1, 0)
    keep = jnp.where(held > 0, 1.0, 0.0)
    merged = jnp.zeros((steps * heads, latent), jnp.float32)
    for s in range(n):
        merged = merged + mix_in[s].astype(jnp.float32) * to_column(shares[s] * keep / whole)
    result = merged.astype(jnp.bfloat16)
    for t in range(steps):
        attended_out[t, 0] = result[t * heads : (t + 1) * heads]

    for d in range(1, n):
        s = peer(d)
        remote(iq_all.at[me], iq_all.at[me], iq_send, iq_recv.at[me], d).wait_send()
        remote(q_all.at[me], q_all.at[me], q_send, q_recv.at[me], d).wait_send()
        remote(cand.at[me], cand.at[me], c_send, c_recv.at[me], d).wait_send()
        remote(mix_out.at[s], mix_in.at[me], m_send, m_recv.at[me], d).wait_send()
        remote(stat_out.at[s], stat_in.at[me], s_send, s_recv.at[me], d).wait_send()


def shards(
    cache, index_key, index_scale, lengths, owners, selected, query, index_query, index_weight
):
    n = lax.axis_size("seq")
    reqs, rows, width = cache.shape
    steps = selected.shape[0]
    heads = query.shape[2]
    iheads, idk = index_query.shape[2:]
    latent = width - ROPE
    fold = max(1, 16 // (steps * reqs))
    f32, bf16 = jnp.float32, jnp.bfloat16
    sems = [pltpu.SemaphoreType.DMA((2,))] + [pltpu.SemaphoreType.DMA((n,))] * 10
    vmem = pl.BlockSpec(memory_space=pltpu.VMEM)
    smem = pl.BlockSpec(memory_space=pltpu.SMEM)
    hbm = pl.BlockSpec(memory_space=pl.ANY)
    out = pl.pallas_call(
        functools.partial(kernel, n),
        out_shape=(
            jax.ShapeDtypeStruct((steps, reqs, rows), f32),
            jax.ShapeDtypeStruct((steps, reqs), f32),
            jax.ShapeDtypeStruct((steps, 1, heads, latent), bf16),
        ),
        in_specs=[smem, smem, hbm, hbm, vmem, vmem, vmem, vmem, vmem],
        out_specs=(vmem, vmem, vmem),
        scratch_shapes=[
            pltpu.VMEM((reqs, width, rows), bf16),
            pltpu.VMEM((reqs, rows, idk), bf16),
            pltpu.VMEM((n, steps * iheads + 16, idk), bf16),
            pltpu.VMEM((n, steps, heads, width), bf16),
            pltpu.VMEM((n, fold * steps * reqs, rows // fold), bf16),
            pltpu.VMEM((reqs, steps, rows), f32),
            pltpu.VMEM((n, steps * heads, latent), bf16),
            pltpu.VMEM((n, 8, steps * heads), f32),
            pltpu.VMEM((n, steps * heads, latent), bf16),
            pltpu.VMEM((n, 8, steps * heads), f32),
        ]
        + sems,
        compiler_params=pltpu.CompilerParams(
            collective_id=0, has_side_effects=True, vmem_limit_bytes=60 * 2**20
        ),
    )(
        lengths,
        owners,
        jnp.swapaxes(cache, 1, 2),
        index_key,
        index_scale,
        selected,
        query,
        index_query,
        index_weight[:, 0],
    )
    return out


def solution(mesh):
    placed = (
        P(("groups", "req"), "seq", None),
        P(("groups", "req"), "seq", None),
        P(("groups", "req"), "seq"),
        P(("groups", "req")),
        P(("groups", "req")),
        P(None, ("groups", "req"), None),
        P(None, ("groups", "seq", "req"), "head", None),
        P(None, ("groups", "seq", "req"), None, None),
        P(None, ("groups", "seq", "req"), None),
    )
    return jax.shard_map(
        shards,
        mesh=mesh,
        in_specs=placed,
        out_specs=(
            P(None, ("groups", "req"), "seq"),
            P(None, ("groups", "req")),
            P(None, ("groups", "seq", "req"), "head", None),
        ),
        check_vma=False,
    )
```

```python
import functools

import jax
import jax.numpy as jnp
from jax import lax
from jax.experimental import pallas as pl
from jax.experimental.pallas import tpu as pltpu
from jax.sharding import PartitionSpec as P

ROPE = 64
LANES = 128
PIVOTS = 7
ROUNDS = 11

score_scale = 192.0 ** (-0.5)
masked_value = -1e30
NT = (((1,), (1,)), ((), ()))
NN = (((1,), (0,)), ((), ()))


def dot(a, b, dims):
    return lax.dot_general(a, b, dims, preferred_element_type=jnp.float32)


def iota(shape, dim):
    return lax.broadcasted_iota(jnp.int32, shape, dim)


def to_column(row):
    n = row.shape[1]
    eye = iota((n, n), 0) == iota((n, n), 1)
    return jnp.sum(jnp.where(eye, row, 0.0), axis=1, keepdims=True)


def to_row(column):
    n = column.shape[0]
    eye = iota((n, n), 0) == iota((n, n), 1)
    return jnp.sum(jnp.where(eye, column, 0.0), axis=0, keepdims=True)


def kernel(
    n,
    lengths,
    owners,
    cache_hbm,
    key_hbm,
    scale_ref,
    selected_ref,
    query_ref,
    iq_ref,
    iw_ref,
    scores_out,
    threshold_out,
    attended_out,
    cache_v,
    key_v,
    iq_all,
    q_all,
    cand,
    bias,
    mix_out,
    stat_out,
    mix_in,
    stat_in,
    local_sem,
    iq_send,
    iq_recv,
    q_send,
    q_left,
    q_recv,
    c_send,
    c_recv,
    m_send,
    m_recv,
    s_send,
    s_recv,
):
    me = lax.axis_index("seq")
    steps, reqs, picks = selected_ref.shape
    rows = cache_v.shape[2]
    heads = query_ref.shape[2]
    latent = mix_in.shape[2]
    iheads = iq_ref.shape[2]
    crow = cand.shape[1]
    fold = crow // (steps * reqs)

    key_copy = pltpu.make_async_copy(key_hbm, key_v, local_sem.at[0])
    cache_copy = pltpu.make_async_copy(cache_hbm, cache_v, local_sem.at[1])
    key_copy.start()
    cache_copy.start()

    def peer(d):
        return lax.rem(me + d, n)

    def remote(src, dst, send, recv, d):
        return pltpu.make_async_remote_copy(
            src_ref=src,
            dst_ref=dst,
            send_sem=send.at[peer(d)],
            recv_sem=recv,
            device_id={"seq": peer(d)},
            device_id_type=pl.DeviceIdType.MESH,
        )

    barrier = pltpu.get_barrier_semaphore()
    for d in range(1, n):
        pl.semaphore_signal(
            barrier, inc=1, device_id={"seq": peer(d)}, device_id_type=pl.DeviceIdType.MESH
        )
    for t in range(steps):
        iq_all[me, t * iheads : (t + 1) * iheads, :] = iq_ref[t, 0]
    wide = iw_ref[...].astype(jnp.float32)
    iq_all[me, steps * iheads :, :] = jnp.pad(
        wide, ((0, 16 - steps), (0, LANES - iheads))
    ).astype(jnp.bfloat16)
    q_all[me] = query_ref[:, 0]
    pl.semaphore_wait(barrier, n - 1)

    for d in range(1, n):
        remote(iq_all.at[me], iq_all.at[me], iq_send, iq_recv.at[me], d).start()
    def hop(shard, to, send):
        return pltpu.make_async_remote_copy(
            src_ref=q_all.at[shard],
            dst_ref=q_all.at[shard],
            send_sem=send.at[shard],
            recv_sem=q_recv.at[shard],
            device_id={"seq": to},
            device_id_type=pl.DeviceIdType.MESH,
        )

    @pl.when(me < n - 1)
    def _():
        hop(me, me + 1, q_send).start()

    @pl.when(me > 0)
    def _():
        hop(me, me - 1, q_left).start()

    base = me * rows
    blocks = rows // LANES
    hi_rows = -(-blocks // 16) * 16
    for j in range(reqs):
        for t in range(steps):
            local = selected_ref[t, j : j + 1, :] - base
            hi = jnp.right_shift(local, 7)
            lo = jnp.bitwise_and(local, LANES - 1)
            hot_hi = jnp.where(iota((hi_rows, picks), 0) == hi, 1.0, 0.0).astype(jnp.bfloat16)
            hot_lo = jnp.where(iota((LANES, picks), 0) == lo, 1.0, 0.0).astype(jnp.bfloat16)
            hits = dot(hot_hi, hot_lo, NT)
            row = jnp.concatenate([hits[b : b + 1] for b in range(blocks)], axis=1)
            bias[j, t : t + 1, :] = jnp.where(row > 0.5, 0.0, masked_value)

    key_copy.wait()
    for d in range(1, n):
        remote(iq_all.at[peer(d)], iq_all.at[peer(d)], iq_send, iq_recv.at[peer(d)], d).wait_recv()
    position = base + iota((1, rows), 1)
    part = rows // fold
    pieces = {}
    for j in range(reqs):
        packed = iq_all[owners[j]]
        dots = jnp.maximum(dot(packed[: steps * iheads], key_v[j], NT), 0.0)
        scale = scale_ref[j : j + 1, :]
        for t in range(steps):
            w = packed[steps * iheads :].astype(jnp.float32)[t : t + 1, :iheads]
            total = jnp.sum(
                dots[t * iheads : (t + 1) * iheads] * to_column(w), axis=0, keepdims=True
            )
            total = total * scale
            inside = position < lengths[j] + t
            scores_out[t, j : j + 1, :] = jnp.where(inside, total, 0.0)
            candidates = jnp.where(inside, total, masked_value)
            for f in range(fold):
                pieces[f * steps * reqs + t * reqs + j] = candidates[:, f * part : (f + 1) * part]
    ordered = [pieces[i] for i in range(crow)]
    cand[me] = jnp.concatenate(ordered, axis=0).astype(jnp.bfloat16)
    for d in range(1, n):
        remote(cand.at[me], cand.at[me], c_send, c_recv.at[me], d).start()

    cache_copy.wait()

    def unit(s):
        j = jnp.int32(0)
        for r in range(reqs):
            j = j + jnp.where(owners[r] == s, r, 0)
        latents = cache_v[j]
        logits = dot(q_all[s].reshape(steps * heads, -1), latents, NN) * score_scale
        mask = bias[j]
        logits = jnp.concatenate(
            [logits[t * heads : (t + 1) * heads] + mask[t : t + 1] for t in range(steps)], axis=0
        )
        peak = jnp.max(logits, axis=1, keepdims=True)
        weights = jnp.exp(logits - peak)
        total = jnp.sum(weights, axis=1, keepdims=True)
        mixture = dot(weights.astype(jnp.bfloat16), latents[:latent], NT) / total
        stat = jnp.concatenate([to_row(peak), to_row(total)], axis=0)
        return mixture.astype(jnp.bfloat16), jnp.pad(stat, ((0, 6), (0, 0)))

    mix_in[me], stat_in[me] = unit(me)

    def send_unit(s, d):
        mix_out[s], stat_out[s] = unit(s)
        remote(mix_out.at[s], mix_in.at[me], m_send, m_recv.at[me], d).start()
        remote(stat_out.at[s], stat_in.at[me], s_send, s_recv.at[me], d).start()

    def distance(d, carry):
        below, above = me - d, me + d

        @pl.when(below >= 0)
        def _():
            hop(below, below, q_send).wait_recv()

            @pl.when(me < n - 1)
            def _():
                hop(below, me + 1, q_send).start()

        @pl.when(above < n)
        def _():
            hop(above, above, q_left).wait_recv()

            @pl.when(me > 0)
            def _():
                hop(above, me - 1, q_left).start()

        @pl.when(below >= 0)
        def _():
            send_unit(below, n - d)

        @pl.when(above < n)
        def _():
            send_unit(above, d)

        return carry

    lax.fori_loop(1, n, distance, 0)

    for d in range(1, n):
        remote(cand.at[peer(d)], cand.at[peer(d)], c_send, c_recv.at[peer(d)], d).wait_recv()
    values = [cand[s].astype(jnp.float32) for s in range(n)]

    def across(x, join):
        own = x
        for f in range(1, fold):
            x = join(x, pltpu.roll(own, f * steps * reqs, 0))
        return x

    def folded(parts, join, reduce):
        x = functools.reduce(join, parts)
        pieces = [x[:, i * LANES : (i + 1) * LANES] for i in range(part // LANES)]
        x = reduce(functools.reduce(join, pieces), axis=1, keepdims=True)
        return across(jnp.broadcast_to(x, (crow, LANES)), join)

    def tile(x):
        return jnp.tile(x, (1, part // LANES))

    highest = folded(values, jnp.maximum, jnp.max)
    lowest = folded(
        [jnp.where(v > 0.5 * masked_value, v, -masked_value) for v in values], jnp.minimum, jnp.min
    )

    def search(_, state):
        low, high = state
        step = (high - low) * (1.0 / (PIVOTS + 1))
        pivots = [low + step * i for i in range(1, PIVOTS + 1)]
        new_low, new_high = low, high
        enough = []
        for pivot in pivots:
            wide_pivot = tile(pivot)
            count = folded(
                [jnp.where(v >= wide_pivot, 1.0, 0.0) for v in values], jnp.add, jnp.sum
            )
            enough.append(count >= picks)
        for pivot, yes in zip(pivots, enough):
            new_low = jnp.where(yes, pivot, new_low)
        for pivot, yes in reversed(list(zip(pivots, enough))):
            new_high = jnp.where(yes, new_high, pivot)
        return new_low, new_high

    low, _ = lax.fori_loop(0, ROUNDS, search, (lowest, highest))
    wide_low = tile(low)
    found = folded(
        [jnp.where(v >= wide_low, v, -masked_value) for v in values], jnp.minimum, jnp.min
    )
    column = found[:, :1]
    for t in range(steps):
        hit = iota((crow, reqs), 0) == t * reqs + iota((crow, reqs), 1)
        threshold_out[t : t + 1, :] = jnp.sum(jnp.where(hit, column, 0.0), axis=0, keepdims=True)

    for d in range(1, n):
        s = peer(d)
        remote(stat_in.at[s], stat_in.at[s], s_send, s_recv.at[s], d).wait_recv()
        remote(mix_in.at[s], mix_in.at[s], m_send, m_recv.at[s], d).wait_recv()
    peaks = [stat_in[s, 0:1, :] for s in range(n)]
    top = functools.reduce(jnp.maximum, peaks)
    shares = [stat_in[s, 1:2, :] * jnp.exp(peaks[s] - top) for s in range(n)]
    whole = functools.reduce(jnp.add, shares)
    held = jnp.int32(0)
    for r in range(reqs):
        held = held + jnp.where(owners[r] == me, 1, 0)
    keep = jnp.where(held > 0, 1.0, 0.0)
    merged = jnp.zeros((steps * heads, latent), jnp.float32)
    for s in range(n):
        merged = merged + mix_in[s].astype(jnp.float32) * to_column(shares[s] * keep / whole)
    result = merged.astype(jnp.bfloat16)
    for t in range(steps):
        attended_out[t, 0] = result[t * heads : (t + 1) * heads]

    for d in range(1, n):
        s = peer(d)
        remote(iq_all.at[me], iq_all.at[me], iq_send, iq_recv.at[me], d).wait_send()
        remote(cand.at[me], cand.at[me], c_send, c_recv.at[me], d).wait_send()
        remote(mix_out.at[s], mix_in.at[me], m_send, m_recv.at[me], d).wait_send()
        remote(stat_out.at[s], stat_in.at[me], s_send, s_recv.at[me], d).wait_send()
    for d in range(n - 1):

        @pl.when((me - d >= 0) & (me < n - 1))
        def _():
            hop(me - d, me + 1, q_send).wait_send()

        @pl.when((me + d < n) & (me > 0))
        def _():
            hop(me + d, me - 1, q_left).wait_send()


def shards(
    cache, index_key, index_scale, lengths, owners, selected, query, index_query, index_weight
):
    n = lax.axis_size("seq")
    reqs, rows, width = cache.shape
    steps = selected.shape[0]
    heads = query.shape[2]
    iheads, idk = index_query.shape[2:]
    latent = width - ROPE
    fold = max(1, 16 // (steps * reqs))
    f32, bf16 = jnp.float32, jnp.bfloat16
    sems = [pltpu.SemaphoreType.DMA((2,))] + [pltpu.SemaphoreType.DMA((n,))] * 11
    vmem = pl.BlockSpec(memory_space=pltpu.VMEM)
    smem = pl.BlockSpec(memory_space=pltpu.SMEM)
    hbm = pl.BlockSpec(memory_space=pl.ANY)
    out = pl.pallas_call(
        functools.partial(kernel, n),
        out_shape=(
            jax.ShapeDtypeStruct((steps, reqs, rows), f32),
            jax.ShapeDtypeStruct((steps, reqs), f32),
            jax.ShapeDtypeStruct((steps, 1, heads, latent), bf16),
        ),
        in_specs=[smem, smem, hbm, hbm, vmem, vmem, vmem, vmem, vmem],
        out_specs=(vmem, vmem, vmem),
        scratch_shapes=[
            pltpu.VMEM((reqs, width, rows), bf16),
            pltpu.VMEM((reqs, rows, idk), bf16),
            pltpu.VMEM((n, steps * iheads + 16, idk), bf16),
            pltpu.VMEM((n, steps, heads, width), bf16),
            pltpu.VMEM((n, fold * steps * reqs, rows // fold), bf16),
            pltpu.VMEM((reqs, steps, rows), f32),
            pltpu.VMEM((n, steps * heads, latent), bf16),
            pltpu.VMEM((n, 8, steps * heads), f32),
            pltpu.VMEM((n, steps * heads, latent), bf16),
            pltpu.VMEM((n, 8, steps * heads), f32),
        ]
        + sems,
        compiler_params=pltpu.CompilerParams(
            collective_id=0, has_side_effects=True, vmem_limit_bytes=53 * 2**20
        ),
    )(
        lengths,
        owners,
        jnp.swapaxes(cache, 1, 2),
        index_key,
        index_scale,
        selected,
        query,
        index_query,
        index_weight[:, 0],
    )
    return out


def solution(mesh):
    placed = (
        P(("groups", "req"), "seq", None),
        P(("groups", "req"), "seq", None),
        P(("groups", "req"), "seq"),
        P(("groups", "req")),
        P(("groups", "req")),
        P(None, ("groups", "req"), None),
        P(None, ("groups", "seq", "req"), "head", None),
        P(None, ("groups", "seq", "req"), None, None),
        P(None, ("groups", "seq", "req"), None),
    )
    return jax.shard_map(
        shards,
        mesh=mesh,
        in_specs=placed,
        out_specs=(
            P(None, ("groups", "req"), "seq"),
            P(None, ("groups", "req")),
            P(None, ("groups", "seq", "req"), "head", None),
        ),
        check_vma=False,
    )
```

```python
import functools

import jax
import jax.numpy as jnp
from jax import lax
from jax.experimental import pallas as pl
from jax.experimental.pallas import tpu as pltpu
from jax.sharding import PartitionSpec as P

ROPE = 64
LANES = 128
PIVOTS = 7
ROUNDS = 11

score_scale = 192.0 ** (-0.5)
masked_value = -1e30
NT = (((1,), (1,)), ((), ()))
NN = (((1,), (0,)), ((), ()))


def dot(a, b, dims):
    return lax.dot_general(a, b, dims, preferred_element_type=jnp.float32)


def iota(shape, dim):
    return lax.broadcasted_iota(jnp.int32, shape, dim)


def to_column(row):
    n = row.shape[1]
    eye = iota((n, n), 0) == iota((n, n), 1)
    return jnp.sum(jnp.where(eye, row, 0.0), axis=1, keepdims=True)


def to_row(column):
    n = column.shape[0]
    eye = iota((n, n), 0) == iota((n, n), 1)
    return jnp.sum(jnp.where(eye, column, 0.0), axis=0, keepdims=True)


def kernel(
    n,
    lengths,
    owners,
    cache_hbm,
    key_hbm,
    scale_ref,
    selected_ref,
    query_ref,
    iq_ref,
    iw_ref,
    scores_out,
    threshold_out,
    attended_out,
    cache_v,
    key_v,
    iq_all,
    q_all,
    cand,
    bias,
    mix_out,
    stat_out,
    mix_in,
    stat_in,
    local_sem,
    iq_send,
    iq_recv,
    q_send,
    q_recv,
    c_send,
    c_recv,
    m_send,
    m_recv,
    s_send,
    s_recv,
):
    me = lax.axis_index("seq")
    steps, reqs, picks = selected_ref.shape
    rows = cache_v.shape[2]
    heads = query_ref.shape[2]
    latent = mix_in.shape[2]
    iheads = iq_ref.shape[2]
    crow = cand.shape[1]
    fold = crow // (steps * reqs)

    key_copy = pltpu.make_async_copy(key_hbm, key_v, local_sem.at[0])
    cache_copy = pltpu.make_async_copy(cache_hbm, cache_v, local_sem.at[1])
    key_copy.start()
    cache_copy.start()

    def peer(d):
        return lax.rem(me + d, n)

    def remote(src, dst, send, recv, d):
        return pltpu.make_async_remote_copy(
            src_ref=src,
            dst_ref=dst,
            send_sem=send.at[peer(d)],
            recv_sem=recv,
            device_id={"seq": peer(d)},
            device_id_type=pl.DeviceIdType.MESH,
        )

    barrier = pltpu.get_barrier_semaphore()
    for d in range(1, n):
        pl.semaphore_signal(
            barrier, inc=1, device_id={"seq": peer(d)}, device_id_type=pl.DeviceIdType.MESH
        )
    for t in range(steps):
        iq_all[me, t * iheads : (t + 1) * iheads, :] = iq_ref[t, 0]
    wide = iw_ref[...].astype(jnp.float32)
    iq_all[me, steps * iheads :, :] = jnp.pad(
        wide, ((0, 16 - steps), (0, LANES - iheads))
    ).astype(jnp.bfloat16)
    q_all[me] = query_ref[:, 0]
    pl.semaphore_wait(barrier, n - 1)

    for d in range(1, n):
        remote(iq_all.at[me], iq_all.at[me], iq_send, iq_recv.at[me], d).start()
    for d in range(1, n):
        remote(q_all.at[me], q_all.at[me], q_send, q_recv.at[me], d).start()

    base = me * rows
    blocks = rows // LANES
    hi_rows = -(-blocks // 16) * 16
    for j in range(reqs):
        for t in range(steps):
            local = selected_ref[t, j : j + 1, :] - base
            hi = jnp.right_shift(local, 7)
            lo = jnp.bitwise_and(local, LANES - 1)
            hot_hi = jnp.where(iota((hi_rows, picks), 0) == hi, 1.0, 0.0).astype(jnp.bfloat16)
            hot_lo = jnp.where(iota((LANES, picks), 0) == lo, 1.0, 0.0).astype(jnp.bfloat16)
            hits = dot(hot_hi, hot_lo, NT)
            row = jnp.concatenate([hits[b : b + 1] for b in range(blocks)], axis=1)
            bias[j, t : t + 1, :] = jnp.where(row > 0.5, 0.0, masked_value)

    key_copy.wait()
    for d in range(1, n):
        remote(iq_all.at[peer(d)], iq_all.at[peer(d)], iq_send, iq_recv.at[peer(d)], d).wait_recv()
    position = base + iota((1, rows), 1)
    part = rows // fold
    pieces = {}
    for j in range(reqs):
        packed = iq_all[owners[j]]
        dots = jnp.maximum(dot(packed[: steps * iheads], key_v[j], NT), 0.0)
        scale = scale_ref[j : j + 1, :]
        for t in range(steps):
            w = packed[steps * iheads :].astype(jnp.float32)[t : t + 1, :iheads]
            total = jnp.sum(
                dots[t * iheads : (t + 1) * iheads] * to_column(w), axis=0, keepdims=True
            )
            total = total * scale
            inside = position < lengths[j] + t
            scores_out[t, j : j + 1, :] = jnp.where(inside, total, 0.0)
            candidates = jnp.where(inside, total, masked_value)
            for f in range(fold):
                pieces[f * steps * reqs + t * reqs + j] = candidates[:, f * part : (f + 1) * part]
    ordered = [pieces[i] for i in range(crow)]
    cand[me] = jnp.concatenate(ordered, axis=0).astype(jnp.bfloat16)
    for d in range(1, n):
        remote(cand.at[me], cand.at[me], c_send, c_recv.at[me], d).start()

    cache_copy.wait()

    def unit(s):
        j = jnp.int32(0)
        for r in range(reqs):
            j = j + jnp.where(owners[r] == s, r, 0)
        latents = cache_v[j]
        logits = dot(q_all[s].reshape(steps * heads, -1), latents, NN) * score_scale
        mask = bias[j]
        logits = jnp.concatenate(
            [logits[t * heads : (t + 1) * heads] + mask[t : t + 1] for t in range(steps)], axis=0
        )
        peak = jnp.max(logits, axis=1, keepdims=True)
        weights = jnp.exp(logits - peak)
        total = jnp.sum(weights, axis=1, keepdims=True)
        mixture = dot(weights.astype(jnp.bfloat16), latents[:latent], NT) / total
        stat = jnp.concatenate([to_row(peak), to_row(total)], axis=0)
        return mixture.astype(jnp.bfloat16), jnp.pad(stat, ((0, 6), (0, 0)))

    mix_in[me], stat_in[me] = unit(me)

    def send_unit(d, carry):
        s = peer(d)
        remote(q_all.at[s], q_all.at[s], q_send, q_recv.at[s], d).wait_recv()
        mix_out[s], stat_out[s] = unit(s)
        remote(mix_out.at[s], mix_in.at[me], m_send, m_recv.at[me], d).start()
        remote(stat_out.at[s], stat_in.at[me], s_send, s_recv.at[me], d).start()
        return carry

    lax.fori_loop(1, n, send_unit, 0)

    for d in range(1, n):
        remote(cand.at[peer(d)], cand.at[peer(d)], c_send, c_recv.at[peer(d)], d).wait_recv()
    values = [cand[s].astype(jnp.float32) for s in range(n)]

    def across(x, join):
        own = x
        for f in range(1, fold):
            x = join(x, pltpu.roll(own, f * steps * reqs, 0))
        return x

    def folded(parts, join, reduce):
        x = functools.reduce(join, parts)
        pieces = [x[:, i * LANES : (i + 1) * LANES] for i in range(part // LANES)]
        x = reduce(functools.reduce(join, pieces), axis=1, keepdims=True)
        return across(jnp.broadcast_to(x, (crow, LANES)), join)

    def tile(x):
        return jnp.tile(x, (1, part // LANES))

    highest = folded(values, jnp.maximum, jnp.max)
    lowest = folded(
        [jnp.where(v > 0.5 * masked_value, v, -masked_value) for v in values], jnp.minimum, jnp.min
    )

    def search(_, state):
        low, high = state
        step = (high - low) * (1.0 / (PIVOTS + 1))
        pivots = [low + step * i for i in range(1, PIVOTS + 1)]
        new_low, new_high = low, high
        enough = []
        for pivot in pivots:
            wide_pivot = tile(pivot)
            count = folded(
                [jnp.where(v >= wide_pivot, 1.0, 0.0) for v in values], jnp.add, jnp.sum
            )
            enough.append(count >= picks)
        for pivot, yes in zip(pivots, enough):
            new_low = jnp.where(yes, pivot, new_low)
        for pivot, yes in reversed(list(zip(pivots, enough))):
            new_high = jnp.where(yes, new_high, pivot)
        return new_low, new_high

    low, _ = lax.fori_loop(0, ROUNDS, search, (lowest, highest))
    wide_low = tile(low)
    found = folded(
        [jnp.where(v >= wide_low, v, -masked_value) for v in values], jnp.minimum, jnp.min
    )
    column = found[:, :1]
    for t in range(steps):
        hit = iota((crow, reqs), 0) == t * reqs + iota((crow, reqs), 1)
        threshold_out[t : t + 1, :] = jnp.sum(jnp.where(hit, column, 0.0), axis=0, keepdims=True)

    for d in range(1, n):
        s = peer(d)
        remote(stat_in.at[s], stat_in.at[s], s_send, s_recv.at[s], d).wait_recv()
        remote(mix_in.at[s], mix_in.at[s], m_send, m_recv.at[s], d).wait_recv()
    peaks = [stat_in[s, 0:1, :] for s in range(n)]
    top = functools.reduce(jnp.maximum, peaks)
    shares = [stat_in[s, 1:2, :] * jnp.exp(peaks[s] - top) for s in range(n)]
    whole = functools.reduce(jnp.add, shares)
    held = jnp.int32(0)
    for r in range(reqs):
        held = held + jnp.where(owners[r] == me, 1, 0)
    keep = jnp.where(held > 0, 1.0, 0.0)
    merged = jnp.zeros((steps * heads, latent), jnp.float32)
    for s in range(n):
        merged = merged + mix_in[s].astype(jnp.float32) * to_column(shares[s] * keep / whole)
    result = merged.astype(jnp.bfloat16)
    for t in range(steps):
        attended_out[t, 0] = result[t * heads : (t + 1) * heads]

    for d in range(1, n):
        s = peer(d)
        remote(iq_all.at[me], iq_all.at[me], iq_send, iq_recv.at[me], d).wait_send()
        remote(q_all.at[me], q_all.at[me], q_send, q_recv.at[me], d).wait_send()
        remote(cand.at[me], cand.at[me], c_send, c_recv.at[me], d).wait_send()
        remote(mix_out.at[s], mix_in.at[me], m_send, m_recv.at[me], d).wait_send()
        remote(stat_out.at[s], stat_in.at[me], s_send, s_recv.at[me], d).wait_send()


def shards(
    cache, index_key, index_scale, lengths, owners, selected, query, index_query, index_weight
):
    n = lax.axis_size("seq")
    reqs, rows, width = cache.shape
    steps = selected.shape[0]
    heads = query.shape[2]
    iheads, idk = index_query.shape[2:]
    latent = width - ROPE
    fold = max(1, 16 // (steps * reqs))
    f32, bf16 = jnp.float32, jnp.bfloat16
    sems = [pltpu.SemaphoreType.DMA((2,))] + [pltpu.SemaphoreType.DMA((n,))] * 10
    vmem = pl.BlockSpec(memory_space=pltpu.VMEM)
    smem = pl.BlockSpec(memory_space=pltpu.SMEM)
    hbm = pl.BlockSpec(memory_space=pl.ANY)
    out = pl.pallas_call(
        functools.partial(kernel, n),
        out_shape=(
            jax.ShapeDtypeStruct((steps, reqs, rows), f32),
            jax.ShapeDtypeStruct((steps, reqs), f32),
            jax.ShapeDtypeStruct((steps, 1, heads, latent), bf16),
        ),
        in_specs=[smem, smem, hbm, hbm, vmem, vmem, vmem, vmem, vmem],
        out_specs=(vmem, vmem, vmem),
        scratch_shapes=[
            pltpu.VMEM((reqs, width, rows), bf16),
            pltpu.VMEM((reqs, rows, idk), bf16),
            pltpu.VMEM((n, steps * iheads + 16, idk), bf16),
            pltpu.VMEM((n, steps, heads, width), bf16),
            pltpu.VMEM((n, fold * steps * reqs, rows // fold), bf16),
            pltpu.VMEM((reqs, steps, rows), f32),
            pltpu.VMEM((n, steps * heads, latent), bf16),
            pltpu.VMEM((n, 8, steps * heads), f32),
            pltpu.VMEM((n, steps * heads, latent), bf16),
            pltpu.VMEM((n, 8, steps * heads), f32),
        ]
        + sems,
        compiler_params=pltpu.CompilerParams(
            collective_id=0, has_side_effects=True, vmem_limit_bytes=53 * 2**20
        ),
    )(
        lengths,
        owners,
        jnp.swapaxes(cache, 1, 2),
        index_key,
        index_scale,
        selected,
        query,
        index_query,
        index_weight[:, 0],
    )
    return out


def solution(mesh):
    placed = (
        P(("groups", "req"), "seq", None),
        P(("groups", "req"), "seq", None),
        P(("groups", "req"), "seq"),
        P(("groups", "req")),
        P(("groups", "req")),
        P(None, ("groups", "req"), None),
        P(None, ("groups", "seq", "req"), "head", None),
        P(None, ("groups", "seq", "req"), None, None),
        P(None, ("groups", "seq", "req"), None),
    )
    return jax.shard_map(
        shards,
        mesh=mesh,
        in_specs=placed,
        out_specs=(
            P(None, ("groups", "req"), "seq"),
            P(None, ("groups", "req")),
            P(None, ("groups", "seq", "req"), "head", None),
        ),
        check_vma=False,
    )
```

```python
import functools

import jax
import jax.numpy as jnp
from jax import lax
from jax.experimental import pallas as pl
from jax.experimental.pallas import tpu as pltpu
from jax.sharding import PartitionSpec as P

ROPE = 64
LANES = 128
PIVOTS = 7
ROUNDS = 11

score_scale = 192.0 ** (-0.5)
masked_value = -1e30
NT = (((1,), (1,)), ((), ()))
NN = (((1,), (0,)), ((), ()))


def dot(a, b, dims):
    return lax.dot_general(a, b, dims, preferred_element_type=jnp.float32)


def iota(shape, dim):
    return lax.broadcasted_iota(jnp.int32, shape, dim)


def to_column(row):
    n = row.shape[1]
    eye = iota((n, n), 0) == iota((n, n), 1)
    return jnp.sum(jnp.where(eye, row, 0.0), axis=1, keepdims=True)


def to_row(column):
    n = column.shape[0]
    eye = iota((n, n), 0) == iota((n, n), 1)
    return jnp.sum(jnp.where(eye, column, 0.0), axis=0, keepdims=True)


def kernel(
    n,
    lengths,
    owners,
    cache_hbm,
    key_hbm,
    scale_ref,
    selected_ref,
    query_ref,
    iq_ref,
    iw_ref,
    scores_out,
    threshold_out,
    attended_out,
    cache_v,
    key_v,
    iq_all,
    q_all,
    cand,
    bias,
    mix_out,
    stat_out,
    mix_in,
    stat_in,
    local_sem,
    iq_send,
    iq_recv,
    q_send,
    q_left,
    q_recv,
    c_send,
    c_recv,
    m_send,
    m_recv,
    s_send,
    s_recv,
):
    me = lax.axis_index("seq")
    steps, reqs, picks = selected_ref.shape
    rows = cache_v.shape[2]
    heads = query_ref.shape[2]
    latent = mix_in.shape[2]
    iheads = iq_ref.shape[2]
    crow = cand.shape[1]
    fold = crow // (steps * reqs)

    key_copy = pltpu.make_async_copy(key_hbm, key_v, local_sem.at[0])
    cache_copy = pltpu.make_async_copy(cache_hbm, cache_v, local_sem.at[1])
    key_copy.start()
    cache_copy.start()

    def peer(d):
        return lax.rem(me + d, n)

    def remote(src, dst, send, recv, d):
        return pltpu.make_async_remote_copy(
            src_ref=src,
            dst_ref=dst,
            send_sem=send.at[peer(d)],
            recv_sem=recv,
            device_id={"seq": peer(d)},
            device_id_type=pl.DeviceIdType.MESH,
        )

    barrier = pltpu.get_barrier_semaphore()
    for d in range(1, n):
        pl.semaphore_signal(
            barrier, inc=1, device_id={"seq": peer(d)}, device_id_type=pl.DeviceIdType.MESH
        )
    for t in range(steps):
        iq_all[me, t * iheads : (t + 1) * iheads, :] = iq_ref[t, 0]
    wide = iw_ref[...].astype(jnp.float32)
    iq_all[me, steps * iheads :, :] = jnp.pad(
        wide, ((0, 16 - steps), (0, LANES - iheads))
    ).astype(jnp.bfloat16)
    q_all[me] = query_ref[:, 0]
    pl.semaphore_wait(barrier, n - 1)

    for d in range(1, n):
        remote(iq_all.at[me], iq_all.at[me], iq_send, iq_recv.at[me], d).start()
    def hop(shard, to, send):
        return pltpu.make_async_remote_copy(
            src_ref=q_all.at[shard],
            dst_ref=q_all.at[shard],
            send_sem=send.at[shard],
            recv_sem=q_recv.at[shard],
            device_id={"seq": to},
            device_id_type=pl.DeviceIdType.MESH,
        )

    @pl.when(me < n - 1)
    def _():
        hop(me, me + 1, q_send).start()

    @pl.when(me > 0)
    def _():
        hop(me, me - 1, q_left).start()

    base = me * rows
    blocks = rows // LANES
    hi_rows = -(-blocks // 16) * 16
    for j in range(reqs):
        for t in range(steps):
            local = selected_ref[t, j : j + 1, :] - base
            hi = jnp.right_shift(local, 7)
            lo = jnp.bitwise_and(local, LANES - 1)
            hot_hi = jnp.where(iota((hi_rows, picks), 0) == hi, 1.0, 0.0).astype(jnp.bfloat16)
            hot_lo = jnp.where(iota((LANES, picks), 0) == lo, 1.0, 0.0).astype(jnp.bfloat16)
            hits = dot(hot_hi, hot_lo, NT)
            row = jnp.concatenate([hits[b : b + 1] for b in range(blocks)], axis=1)
            bias[j, t : t + 1, :] = jnp.where(row > 0.5, 0.0, masked_value)

    key_copy.wait()
    for d in range(1, n):
        remote(iq_all.at[peer(d)], iq_all.at[peer(d)], iq_send, iq_recv.at[peer(d)], d).wait_recv()
    position = base + iota((1, rows), 1)
    part = rows // fold
    pieces = {}
    for j in range(reqs):
        packed = iq_all[owners[j]]
        dots = jnp.maximum(dot(packed[: steps * iheads], key_v[j], NT), 0.0)
        scale = scale_ref[j : j + 1, :]
        for t in range(steps):
            w = packed[steps * iheads :].astype(jnp.float32)[t : t + 1, :iheads]
            total = jnp.sum(
                dots[t * iheads : (t + 1) * iheads] * to_column(w), axis=0, keepdims=True
            )
            total = total * scale
            inside = position < lengths[j] + t
            scores_out[t, j : j + 1, :] = jnp.where(inside, total, 0.0)
            candidates = jnp.where(inside, total, masked_value)
            for f in range(fold):
                pieces[f * steps * reqs + t * reqs + j] = candidates[:, f * part : (f + 1) * part]
    ordered = [pieces[i] for i in range(crow)]
    cand[me] = jnp.concatenate(ordered, axis=0).astype(jnp.bfloat16)
    for d in range(1, n):
        remote(cand.at[me], cand.at[me], c_send, c_recv.at[me], d).start()

    cache_copy.wait()

    def unit(s):
        j = jnp.int32(0)
        for r in range(reqs):
            j = j + jnp.where(owners[r] == s, r, 0)
        latents = cache_v[j]
        logits = dot(q_all[s].reshape(steps * heads, -1), latents, NN) * score_scale
        mask = bias[j]
        logits = jnp.concatenate(
            [logits[t * heads : (t + 1) * heads] + mask[t : t + 1] for t in range(steps)], axis=0
        )
        peak = jnp.max(logits, axis=1, keepdims=True)
        weights = jnp.exp(logits - peak)
        total = jnp.sum(weights, axis=1, keepdims=True)
        mixture = dot(weights.astype(jnp.bfloat16), latents[:latent], NT) / total
        stat = jnp.concatenate([to_row(peak), to_row(total)], axis=0)
        return mixture.astype(jnp.bfloat16), jnp.pad(stat, ((0, 6), (0, 0)))

    mix_in[me], stat_in[me] = unit(me)

    def send_unit(s, d):
        mix_out[s], stat_out[s] = unit(s)
        remote(mix_out.at[s], mix_in.at[me], m_send, m_recv.at[me], d).start()
        remote(stat_out.at[s], stat_in.at[me], s_send, s_recv.at[me], d).start()

    def distance(d, carry):
        below, above = me - d, me + d

        @pl.when(below >= 0)
        def _():
            hop(below, below, q_send).wait_recv()

            @pl.when(me < n - 1)
            def _():
                hop(below, me + 1, q_send).start()

        @pl.when(above < n)
        def _():
            hop(above, above, q_left).wait_recv()

            @pl.when(me > 0)
            def _():
                hop(above, me - 1, q_left).start()

        @pl.when(below >= 0)
        def _():
            send_unit(below, n - d)

        @pl.when(above < n)
        def _():
            send_unit(above, d)

        return carry

    lax.fori_loop(1, n, distance, 0)

    for d in range(1, n):
        remote(cand.at[peer(d)], cand.at[peer(d)], c_send, c_recv.at[peer(d)], d).wait_recv()
    values = [cand[s].astype(jnp.float32) for s in range(n)]

    def across(x, join):
        own = x
        for f in range(1, fold):
            x = join(x, pltpu.roll(own, f * steps * reqs, 0))
        return x

    def folded(parts, join, reduce):
        x = functools.reduce(join, parts)
        pieces = [x[:, i * LANES : (i + 1) * LANES] for i in range(part // LANES)]
        x = reduce(functools.reduce(join, pieces), axis=1, keepdims=True)
        return across(jnp.broadcast_to(x, (crow, LANES)), join)

    def tile(x):
        return jnp.tile(x, (1, part // LANES))

    highest = folded(values, jnp.maximum, jnp.max)
    lowest = folded(
        [jnp.where(v > 0.5 * masked_value, v, -masked_value) for v in values], jnp.minimum, jnp.min
    )

    def search(_, state):
        low, high = state
        step = (high - low) * (1.0 / (PIVOTS + 1))
        pivots = [low + step * i for i in range(1, PIVOTS + 1)]
        new_low, new_high = low, high
        enough = []
        for pivot in pivots:
            wide_pivot = tile(pivot)
            count = folded(
                [jnp.where(v >= wide_pivot, 1.0, 0.0) for v in values], jnp.add, jnp.sum
            )
            enough.append(count >= picks)
        for pivot, yes in zip(pivots, enough):
            new_low = jnp.where(yes, pivot, new_low)
        for pivot, yes in reversed(list(zip(pivots, enough))):
            new_high = jnp.where(yes, new_high, pivot)
        return new_low, new_high

    low, _ = lax.fori_loop(0, ROUNDS, search, (lowest, highest))
    wide_low = tile(low)
    found = folded(
        [jnp.where(v >= wide_low, v, -masked_value) for v in values], jnp.minimum, jnp.min
    )
    column = found[:, :1]
    for t in range(steps):
        hit = iota((crow, reqs), 0) == t * reqs + iota((crow, reqs), 1)
        threshold_out[t : t + 1, :] = jnp.sum(jnp.where(hit, column, 0.0), axis=0, keepdims=True)

    for d in range(1, n):
        s = peer(d)
        remote(stat_in.at[s], stat_in.at[s], s_send, s_recv.at[s], d).wait_recv()
        remote(mix_in.at[s], mix_in.at[s], m_send, m_recv.at[s], d).wait_recv()
    peaks = [stat_in[s, 0:1, :] for s in range(n)]
    top = functools.reduce(jnp.maximum, peaks)
    shares = [stat_in[s, 1:2, :] * jnp.exp(peaks[s] - top) for s in range(n)]
    whole = functools.reduce(jnp.add, shares)
    held = jnp.int32(0)
    for r in range(reqs):
        held = held + jnp.where(owners[r] == me, 1, 0)
    keep = jnp.where(held > 0, 1.0, 0.0)
    merged = jnp.zeros((steps * heads, latent), jnp.float32)
    for s in range(n):
        merged = merged + mix_in[s].astype(jnp.float32) * to_column(shares[s] * keep / whole)
    result = merged.astype(jnp.bfloat16)
    for t in range(steps):
        attended_out[t, 0] = result[t * heads : (t + 1) * heads]

    for d in range(1, n):
        s = peer(d)
        remote(iq_all.at[me], iq_all.at[me], iq_send, iq_recv.at[me], d).wait_send()
        remote(cand.at[me], cand.at[me], c_send, c_recv.at[me], d).wait_send()
        remote(mix_out.at[s], mix_in.at[me], m_send, m_recv.at[me], d).wait_send()
        remote(stat_out.at[s], stat_in.at[me], s_send, s_recv.at[me], d).wait_send()
    for d in range(n - 1):

        @pl.when((me - d >= 0) & (me < n - 1))
        def _():
            hop(me - d, me + 1, q_send).wait_send()

        @pl.when((me + d < n) & (me > 0))
        def _():
            hop(me + d, me - 1, q_left).wait_send()


def shards(
    cache, index_key, index_scale, lengths, owners, selected, query, index_query, index_weight
):
    n = lax.axis_size("seq")
    reqs, rows, width = cache.shape
    steps = selected.shape[0]
    heads = query.shape[2]
    iheads, idk = index_query.shape[2:]
    latent = width - ROPE
    fold = max(1, 16 // (steps * reqs))
    f32, bf16 = jnp.float32, jnp.bfloat16
    sems = [pltpu.SemaphoreType.DMA((2,))] + [pltpu.SemaphoreType.DMA((n,))] * 11
    vmem = pl.BlockSpec(memory_space=pltpu.VMEM)
    smem = pl.BlockSpec(memory_space=pltpu.SMEM)
    hbm = pl.BlockSpec(memory_space=pl.ANY)
    out = pl.pallas_call(
        functools.partial(kernel, n),
        out_shape=(
            jax.ShapeDtypeStruct((steps, reqs, rows), f32),
            jax.ShapeDtypeStruct((steps, reqs), f32),
            jax.ShapeDtypeStruct((steps, 1, heads, latent), bf16),
        ),
        in_specs=[smem, smem, hbm, hbm, vmem, vmem, vmem, vmem, vmem],
        out_specs=(vmem, vmem, vmem),
        scratch_shapes=[
            pltpu.VMEM((reqs, width, rows), bf16),
            pltpu.VMEM((reqs, rows, idk), bf16),
            pltpu.VMEM((n, steps * iheads + 16, idk), bf16),
            pltpu.VMEM((n, steps, heads, width), bf16),
            pltpu.VMEM((n, fold * steps * reqs, rows // fold), bf16),
            pltpu.VMEM((reqs, steps, rows), f32),
            pltpu.VMEM((n, steps * heads, latent), bf16),
            pltpu.VMEM((n, 8, steps * heads), f32),
            pltpu.VMEM((n, steps * heads, latent), bf16),
            pltpu.VMEM((n, 8, steps * heads), f32),
        ]
        + sems,
        compiler_params=pltpu.CompilerParams(
            collective_id=0, has_side_effects=True, vmem_limit_bytes=60 * 2**20
        ),
    )(
        lengths,
        owners,
        jnp.swapaxes(cache, 1, 2),
        index_key,
        index_scale,
        selected,
        query,
        index_query,
        index_weight[:, 0],
    )
    return out


def solution(mesh):
    placed = (
        P(("groups", "req"), "seq", None),
        P(("groups", "req"), "seq", None),
        P(("groups", "req"), "seq"),
        P(("groups", "req")),
        P(("groups", "req")),
        P(None, ("groups", "req"), None),
        P(None, ("groups", "seq", "req"), "head", None),
        P(None, ("groups", "seq", "req"), None, None),
        P(None, ("groups", "seq", "req"), None),
    )
    return jax.shard_map(
        shards,
        mesh=mesh,
        in_specs=placed,
        out_specs=(
            P(None, ("groups", "req"), "seq"),
            P(None, ("groups", "req")),
            P(None, ("groups", "seq", "req"), "head", None),
        ),
        check_vma=False,
    )
```
